512 devices in a mesh: ctx: 64 (over y, z_lo, core), head: 8 (over x, z_hi).
Axes of the slice: x: 4, y: 4, z: 16 (z_hi: 2, z_lo: 8; z = z_hi * 8 + z_lo), core: 2. Of those that a mesh axis runs over, the one named last changes fastest.
Arguments:
- q_first: bfloat16 [1024, 1024], P('ctx', 'head'), may hold values from -8 to 8
- q_second: bfloat16 [1024, 1024], P('ctx', 'head'), may hold values from -8 to 8
- grad_out: bfloat16 [1024, 2048], P('ctx', 'head'), may hold values from -6 to 6
- k_first: bfloat16 [65536, 1024], P('ctx', 'head'), may hold values from -4.5 to 4.5
- k_second: bfloat16 [65536, 1024], P('ctx', 'head'), may hold values from -4.5 to 4.5
- values: bfloat16 [65536, 2048], P('ctx', 'head'), may hold values from -6 to 6
- w_query: bfloat16 [4096, 2048], P(None, 'head'), may hold values from -0.09375 to 0.09375
- block_offsets: int32 [64], replicated, may hold values from 0 to 4095, as said below
- lambda_full: float32 [1], replicated, may hold values from 0.2 to 0.8
Outputs:
- grad_q_first: bfloat16 [1024, 1024], P('ctx', 'head')
- grad_q_second: bfloat16 [1024, 1024], P('ctx', 'head')
- grad_k_first: bfloat16 [65536, 1024], P('ctx', 'head')
- grad_k_second: bfloat16 [65536, 1024], P('ctx', 'head')
- grad_values: bfloat16 [65536, 2048], P('ctx', 'head')
- grad_slab_input: bfloat16 [1024, 4096], P('ctx', 'head')
The draws below stay inside these ranges and needn't reach their ends.
Inputs may be any that keep to these rules, and one draw needn't show every extreme that they name: block_offsets[b] lies in [b * 64, (b + 1) * 64); the first is 0 and the last is 4095.
All inputs are finite; a program needn't handle non-finite values.
Results may differ from the reference program's by a relative error of at most 0.015.
Values may be sent and summed in bfloat16 or wider, within the bound.
No kernel may reach another device: no remote copies, remote signals or barrier semaphores. Data moves between devices by JAX's collectives and lax.ppermute only.
A program may use at most 64 MiB of HBM per device.

```python
import jax
import jax.numpy as jnp
from jax import lax

D = 4096
DH = 128
HP = 8
KL = 1024
QL = 16
QBLOCKS = 64
QS = 1024
TOKENS = 65536


def query_rows(key, which):
    key = jax.random.fold_in(key, 10 + which)
    base = jnp.clip(3.0 * jax.random.normal(key, (QS, HP * DH), jnp.float32), -8.0, 8.0)
    signs = (2 * jax.random.randint(jax.random.fold_in(key, 7), (QS, HP * DH), 0, 2) - 1).astype(jnp.float32)
    loud = (jnp.arange(QS) % 8 == 5)[:, None]
    base = jnp.where(loud, 8.0 * signs, base)
    return base.astype(jnp.bfloat16)


def key_rows(key, which):
    key = jax.random.fold_in(key, 20 + which)
    base = jnp.clip(jax.random.normal(key, (TOKENS, HP * DH), jnp.float32), -4.5, 4.5)
    return base.astype(jnp.bfloat16)


def draw_q_first(key, part):
    return query_rows(key, 1)


def draw_q_second(key, part):
    return query_rows(key, 2)


def draw_k_first(key, part):
    return key_rows(key, 1)


def draw_k_second(key, part):
    return key_rows(key, 2)


def draw_block_offsets(key, part):
    key = jax.random.fold_in(key, 5)
    per_device = KL // QL
    picked = jax.random.randint(key, (QBLOCKS,), 0, per_device)
    picked = picked.at[0].set(0).at[QBLOCKS - 1].set(per_device - 1)
    return (jnp.arange(QBLOCKS, dtype=jnp.int32) * per_device + picked).astype(jnp.int32)


def steps_of(own_key, dims, split, low, high):
    level = 1.0
    for dim, shards_of in split:
        draws = jax.random.uniform(jax.random.fold_in(jax.random.fold_in(own_key, 6), dim), (shards_of,), jnp.float32, low / len(split), high / len(split))
        level = level * jnp.repeat(jnp.exp(draws), dims[dim] // shards_of).reshape((-1,) + (1,) * (len(dims) - 1 - dim))
    return level


def gaussian(key, dims, deviation, most, shards=(), kind=jnp.bfloat16):
    result = deviation * jax.random.normal(key, dims, jnp.float32)
    if shards:
        result = result * steps_of(key, dims, shards, -0.22, 0.18)
    return jnp.clip(result, -most, most).astype(kind)


def setup_inputs(seed: int = 0) -> dict:
    seeds = jax.random.split(jax.random.key(seed), 10)
    return {
        "q_first": draw_q_first(jax.random.fold_in(seeds[9], 71), 0),
        "q_second": draw_q_second(jax.random.fold_in(seeds[9], 71), 0),
        "grad_out": gaussian(seeds[2], (QS, HP * 2 * DH), 1.0, 6.0, ((0, 64), (1, 8))),
        "k_first": draw_k_first(jax.random.fold_in(seeds[9], 71), 0),
        "k_second": draw_k_second(jax.random.fold_in(seeds[9], 71), 0),
        "values": gaussian(seeds[5], (TOKENS, HP * 2 * DH), 1.0, 6.0, ((0, 64), (1, 8))),
        "w_query": gaussian(seeds[6], (D, HP * 2 * DH), D ** -0.5, 0.09375, ((1, 8),)),
        "block_offsets": draw_block_offsets(jax.random.fold_in(seeds[9], 71), 0),
        "lambda_full": jnp.clip(jax.random.uniform(seeds[8], (1,), jnp.float32, 0.2, 0.8), 0.2, 0.8),
    }


NEG = -1.0e30


def pair_grads(inputs, weight, query_pos):
    q_one, q_two, cotangent, k_one, k_two, vals = inputs
    scale = DH ** -0.5
    key_pos = jnp.arange(TOKENS, dtype=jnp.int32)
    block = 512 if QS % 512 == 0 else QS
    count = QS // block

    def step(carry, piece):
        grad_ka, grad_kb, grad_val = carry
        part_a, part_b, part_grad, positions = piece
        visible = key_pos[None, :] <= positions[:, None]

        def probs(queries, keys):
            logits = jnp.dot(queries, keys.T, preferred_element_type=jnp.float32) * scale
            logits = jnp.where(visible, logits, NEG)
            expo = jnp.where(visible, jnp.exp(logits - jnp.max(logits, axis=1, keepdims=True)), 0.0)
            return expo / jnp.sum(expo, axis=1, keepdims=True)

        prob_a = probs(part_a, k_one)
        prob_b = probs(part_b, k_two)
        product = jnp.dot(part_grad, vals.T, preferred_element_type=jnp.float32)
        delta_a = jnp.sum(prob_a * product, axis=1, keepdims=True)
        delta_b = jnp.sum(prob_b * product, axis=1, keepdims=True)
        mixed = (prob_a - weight * prob_b).astype(jnp.bfloat16)
        slope_a = (prob_a * (product - delta_a) * scale).astype(jnp.bfloat16)
        slope_b = (-weight * prob_b * (product - delta_b) * scale).astype(jnp.bfloat16)
        grad_val = grad_val + jnp.dot(mixed.T, part_grad, preferred_element_type=jnp.float32)
        grad_ka = grad_ka + jnp.dot(slope_a.T, part_a, preferred_element_type=jnp.float32)
        grad_kb = grad_kb + jnp.dot(slope_b.T, part_b, preferred_element_type=jnp.float32)
        query_part = jnp.concatenate([jnp.dot(slope_a, k_one, preferred_element_type=jnp.float32), jnp.dot(slope_b, k_two, preferred_element_type=jnp.float32)], axis=1)
        return (grad_ka, grad_kb, grad_val), query_part

    pieces = (q_one.reshape(count, block, DH), q_two.reshape(count, block, DH), cotangent.reshape(count, block, 2 * DH), query_pos.reshape(count, block))
    start = (jnp.zeros((TOKENS, DH), jnp.float32), jnp.zeros((TOKENS, DH), jnp.float32), jnp.zeros((TOKENS, 2 * DH), jnp.float32))
    (grad_ka, grad_kb, grad_val), query_grad = lax.scan(step, start, pieces)
    return query_grad.reshape(QS, 2 * DH), grad_ka, grad_kb, grad_val


def split_heads(array, width):
    return array.reshape(array.shape[0], HP, width).transpose(1, 0, 2)


def join_heads(array):
    return array.transpose(1, 0, 2).reshape(array.shape[1], array.shape[0] * array.shape[2])


def reference(q_first, q_second, grad_out, k_first, k_second, values, w_query, block_offsets, lambda_full):
    weight = lambda_full[0]
    query_pos = (block_offsets[:, None] * QL + jnp.arange(QL, dtype=jnp.int32)[None, :]).reshape(QS).astype(jnp.int32)
    stacked = (split_heads(q_first, DH), split_heads(q_second, DH), split_heads(grad_out, 2 * DH), split_heads(k_first, DH), split_heads(k_second, DH), split_heads(values, 2 * DH))
    query_grad, grad_ka, grad_kb, grad_val = lax.map(lambda inputs: pair_grads(inputs, weight, query_pos), stacked)
    query_low = query_grad.astype(jnp.bfloat16)
    weights = w_query.reshape(D, HP, 2 * DH).transpose(1, 0, 2)
    terms = jnp.einsum("hqe,hde->hqd", query_low.astype(jnp.float32), weights.astype(jnp.float32)).astype(jnp.bfloat16)
    terms = lax.optimization_barrier(terms)
    slab = jnp.sum(terms.astype(jnp.float32), axis=0).astype(jnp.bfloat16)
    grad_q_first = join_heads(query_low[:, :, :DH])
    grad_q_second = join_heads(query_low[:, :, DH:])
    return (grad_q_first, grad_q_second, join_heads(grad_ka).astype(jnp.bfloat16), join_heads(grad_kb).astype(jnp.bfloat16), join_heads(grad_val).astype(jnp.bfloat16), slab)
```

```python
import jax
import jax.numpy as jnp
from jax import lax
from jax.experimental import pallas as pl
from jax.experimental.pallas import tpu as pltpu
from jax.sharding import Mesh, PartitionSpec as P

NEG = -1e30
KEY_TILE = 256
ROW_TILE = 256
VMEM = pltpu.CompilerParams(
    dimension_semantics=("arbitrary",), vmem_limit_bytes=40 * 1024 * 1024
)

MAPS = (0, 4)


def outer(left, right):
    return lax.dot_general(
        left, right, (((1,), (1,)), ((), ())), preferred_element_type=jnp.float32
    )


def matmul(left, right):
    return jnp.dot(left, right, preferred_element_type=jnp.float32)


def matmul_first(left, right):
    return lax.dot_general(
        left, right, (((0,), (0,)), ((), ())), preferred_element_type=jnp.float32
    )


def tiles(total, size):
    size = min(size, total)
    return [(start, size) for start in range(0, total, size)]


def stats_kernel(base_ref, pos_ref, every_ref, k_one_ref, k_two_ref, val_ref, stats_ref):
    head_dim = k_one_ref.shape[1]
    scale = head_dim**-0.5
    tile = k_one_ref.shape[0]
    step = pl.program_id(0)

    @pl.when(step == 0)
    def _():
        row = lax.broadcasted_iota(jnp.int32, stats_ref.shape, 0)
        stats_ref[...] = jnp.where((row == 0) | (row == 4), NEG, 0.0)

    base = base_ref[0] + step * tile
    for start, width in tiles(every_ref.shape[0], ROW_TILE):
        span = slice(start, start + width)
        key_pos = base + lax.broadcasted_iota(jnp.int32, (tile, width), 0)
        visible = key_pos <= pos_ref[:, span]
        product = outer(val_ref[...], every_ref[span, 2 * head_dim :])
        for row, k_ref, offset in ((0, k_one_ref, 0), (4, k_two_ref, head_dim)):
            logits = outer(k_ref[...], every_ref[span, offset : offset + head_dim]) * scale
            logits = jnp.where(visible, logits, NEG)
            before = stats_ref[row : row + 1, span]
            top = jnp.maximum(before, jnp.max(logits, axis=0, keepdims=True))
            expo = jnp.exp(logits - top)
            kept = jnp.exp(before - top)
            stats_ref[row : row + 1, span] = top
            stats_ref[row + 1 : row + 2, span] = stats_ref[
                row + 1 : row + 2, span
            ] * kept + jnp.sum(expo, axis=0, keepdims=True)
            stats_ref[row + 2 : row + 3, span] = stats_ref[
                row + 2 : row + 3, span
            ] * kept + jnp.sum(expo * product, axis=0, keepdims=True)


def grad_kernel(
    base_ref,
    lam_ref,
    pos_ref,
    stats_ref,
    every_ref,
    k_one_ref,
    k_two_ref,
    val_ref,
    dk_one_ref,
    dk_two_ref,
    dval_ref,
    dq_ref,
    final_ref,
    acc_ref,
):
    head_dim = k_one_ref.shape[1]
    scale = head_dim**-0.5
    tile = k_one_ref.shape[0]
    step = pl.program_id(0)
    lam = lam_ref[0]

    @pl.when(step == 0)
    def _():
        for row in MAPS:
            top = jnp.max(stats_ref[:, row, :], axis=0, keepdims=True)
            total = jnp.zeros_like(top)
            mix = jnp.zeros_like(top)
            for part in range(stats_ref.shape[0]):
                kept = jnp.exp(stats_ref[part, row : row + 1, :] - top)
                total = total + kept * stats_ref[part, row + 1 : row + 2, :]
                mix = mix + kept * stats_ref[part, row + 2 : row + 3, :]
            final_ref[row : row + 1, :] = top + jnp.log(total)
            final_ref[row + 1 : row + 2, :] = mix / total
        acc_ref[...] = jnp.zeros_like(acc_ref)

    base = base_ref[0] + step * tile
    grad_one = jnp.zeros((tile, head_dim), jnp.float32)
    grad_two = jnp.zeros((tile, head_dim), jnp.float32)
    grad_val = jnp.zeros((tile, 2 * head_dim), jnp.float32)
    for start, width in tiles(every_ref.shape[0], ROW_TILE):
        span = slice(start, start + width)
        key_pos = base + lax.broadcasted_iota(jnp.int32, (tile, width), 0)
        visible = key_pos <= pos_ref[:, span]
        q_one = every_ref[span, :head_dim]
        q_two = every_ref[span, head_dim : 2 * head_dim]
        cotangent = every_ref[span, 2 * head_dim :]
        product = outer(val_ref[...], cotangent)
        logits_one = jnp.where(visible, outer(k_one_ref[...], q_one) * scale, NEG)
        logits_two = jnp.where(visible, outer(k_two_ref[...], q_two) * scale, NEG)
        prob_one = jnp.exp(logits_one - final_ref[0:1, span])
        prob_two = jnp.exp(logits_two - final_ref[4:5, span]) * lam
        mixed = (prob_one - prob_two).astype(jnp.bfloat16)
        slope_one = (prob_one * (product - final_ref[1:2, span]) * scale).astype(jnp.bfloat16)
        slope_two = (prob_two * (final_ref[5:6, span] - product) * scale).astype(jnp.bfloat16)
        grad_val = grad_val + matmul(mixed, cotangent)
        grad_one = grad_one + matmul(slope_one, q_one)
        grad_two = grad_two + matmul(slope_two, q_two)
        acc_ref[span, :head_dim] += matmul_first(slope_one, k_one_ref[...])
        acc_ref[span, head_dim:] += matmul_first(slope_two, k_two_ref[...])
    dk_one_ref[...] = grad_one.astype(jnp.bfloat16)
    dk_two_ref[...] = grad_two.astype(jnp.bfloat16)
    dval_ref[...] = grad_val.astype(jnp.bfloat16)

    @pl.when(step == pl.num_programs(0) - 1)
    def _():
        dq_ref[...] = acc_ref[...].astype(jnp.bfloat16)


def whole(shape):
    return pl.BlockSpec(shape, lambda step: (0,) * len(shape))


def keyed(width):
    return pl.BlockSpec((KEY_TILE, width), lambda step: (step, 0))


def local_stats(base, positions, every, k_first, k_second, values):
    rows, keys, head_dim = every.shape[0], k_first.shape[0], k_first.shape[1]
    smem = pl.BlockSpec(memory_space=pltpu.SMEM)
    return pl.pallas_call(
        stats_kernel,
        grid=(keys // KEY_TILE,),
        out_shape=jax.ShapeDtypeStruct((8, rows), jnp.float32),
        in_specs=[
            smem,
            whole((1, rows)),
            whole(every.shape),
            keyed(head_dim),
            keyed(head_dim),
            keyed(2 * head_dim),
        ],
        out_specs=whole((8, rows)),
        compiler_params=VMEM,
        cost_estimate=pl.CostEstimate(
            flops=8 * rows * keys * head_dim,
            bytes_accessed=2 * 4 * head_dim * (rows + keys),
            transcendentals=2 * rows * keys,
        ),
    )(base, positions, every, k_first, k_second, values)


def local_grads(base, lam, positions, stats, every, k_first, k_second, values):
    rows, keys, head_dim = every.shape[0], k_first.shape[0], k_first.shape[1]
    smem = pl.BlockSpec(memory_space=pltpu.SMEM)
    low = jnp.bfloat16
    return pl.pallas_call(
        grad_kernel,
        grid=(keys // KEY_TILE,),
        out_shape=(
            jax.ShapeDtypeStruct((keys, head_dim), low),
            jax.ShapeDtypeStruct((keys, head_dim), low),
            jax.ShapeDtypeStruct((keys, 2 * head_dim), low),
            jax.ShapeDtypeStruct((rows, 2 * head_dim), low),
        ),
        in_specs=[
            smem,
            smem,
            whole((1, rows)),
            whole(stats.shape),
            whole(every.shape),
            keyed(head_dim),
            keyed(head_dim),
            keyed(2 * head_dim),
        ],
        out_specs=(
            keyed(head_dim),
            keyed(head_dim),
            keyed(2 * head_dim),
            whole((rows, 2 * head_dim)),
        ),
        scratch_shapes=[
            pltpu.VMEM((8, rows), jnp.float32),
            pltpu.VMEM((rows, 2 * head_dim), jnp.float32),
        ],
        compiler_params=VMEM,
        cost_estimate=pl.CostEstimate(
            flops=20 * rows * keys * head_dim,
            bytes_accessed=2 * 4 * head_dim * (rows + 2 * keys),
            transcendentals=2 * rows * keys,
        ),
    )(base, lam, positions, stats, every, k_first, k_second, values)


def spread(value, axes):
    copies = jnp.broadcast_to(value[None], (lax.axis_size(axes),) + value.shape)
    return lax.all_to_all(copies, axes, 0, 0)


def fold_kernel(one_ref, two_ref, out_ref):
    out_ref[...] = jnp.zeros_like(out_ref)
    for row in MAPS:
        one, two = one_ref[row : row + 1, :], two_ref[row : row + 1, :]
        top = jnp.maximum(one, two)
        left, right = jnp.exp(one - top), jnp.exp(two - top)
        out_ref[row : row + 1, :] = top
        for item in (row + 1, row + 2):
            out_ref[item : item + 1, :] = (
                one_ref[item : item + 1, :] * left + two_ref[item : item + 1, :] * right
            )


def fold(one, two):
    return pl.pallas_call(fold_kernel, out_shape=jax.ShapeDtypeStruct(one.shape, one.dtype))(
        one, two
    )


def body(sizes, q_first, q_second, grad_out, k_first, k_second, values, w_query, offsets, lam):
    rows_own, head_dim = q_first.shape
    keys_own = k_first.shape[0]
    y, z, core = (sizes[name] for name in ("y", "z", "core"))
    rows = y * z * core * rows_own
    base = (lax.axis_index(("y", "z", "core")) * keys_own).astype(jnp.int32).reshape(1)
    starts = offsets.reshape(y, z, core).transpose(0, 2, 1).reshape(-1, 1) * rows_own
    positions = (starts + jnp.arange(rows_own, dtype=jnp.int32)[None, :]).reshape(1, rows)

    own = jnp.concatenate([q_first, q_second, grad_out], axis=1)
    every = spread(spread(own, "z"), ("y", "core")).reshape(rows, 4 * head_dim)

    stats = local_stats(base, positions, every, k_first, k_second, values)
    for name in ("core", "y"):
        size = sizes[name]
        reach = 1
        while reach < size:
            pairs = [(i, i ^ reach) for i in range(size)]
            stats = fold(stats, lax.ppermute(stats, name, pairs))
            reach *= 2
    stats = spread(stats, "z")

    dk_first, dk_second, dval, dq = local_grads(
        base, lam, positions, stats, every, k_first, k_second, values
    )

    dq = dq.reshape(y * core, z * rows_own, 2 * head_dim)
    dq = lax.all_to_all(dq, ("y", "core"), 0, 0)
    dq = jnp.sum(dq.astype(jnp.float32), axis=0).astype(jnp.bfloat16)
    dq = lax.all_to_all(dq.reshape(z, rows_own, 2 * head_dim), "z", 0, 0)
    dq = jnp.sum(dq.astype(jnp.float32), axis=0).astype(jnp.bfloat16)

    heads = sizes["head"]
    columns = w_query.reshape(heads, w_query.shape[0] // heads, 2 * head_dim)
    term = jnp.einsum("qe,hde->hqd", dq, columns, preferred_element_type=jnp.float32)
    term = lax.all_to_all(term.astype(jnp.bfloat16), "head", 0, 0)
    slab = jnp.sum(term.astype(jnp.float32), axis=0).astype(jnp.bfloat16)
    return dq[:, :head_dim], dq[:, head_dim:], dk_first, dk_second, dval, slab


def build(mesh, y, z, core):
    names = ("y", "z", "core", "head")
    fine = Mesh(mesh.devices.reshape(y, z, core, mesh.shape["head"]), names)
    sizes = dict(zip(names, fine.devices.shape))
    cut = P(("y", "z", "core"), "head")

    def run(*args):
        return body(sizes, *args)

    return jax.shard_map(
        run,
        mesh=fine,
        in_specs=(cut,) * 6 + (P(None, "head"), P(), P()),
        out_specs=(cut,) * 6,
        check_vma=False,
    )


def solution(mesh):
    return build(mesh, 4, 8, 2)
```

```python
import jax
import jax.numpy as jnp
from jax import lax
from jax.experimental import pallas as pl
from jax.experimental.pallas import tpu as pltpu
from jax.sharding import Mesh, PartitionSpec as P

NEG = -1e30
KEY_TILE = 256
ROW_TILE = 256
VMEM = pltpu.CompilerParams(vmem_limit_bytes=58 * 1024 * 1024)

STATS = 4


def outer(left, right):
    return lax.dot_general(
        left, right, (((1,), (1,)), ((), ())), preferred_element_type=jnp.float32
    )


def matmul(left, right):
    return jnp.dot(left, right, preferred_element_type=jnp.float32)


def matmul_first(left, right):
    return lax.dot_general(
        left, right, (((0,), (0,)), ((), ())), preferred_element_type=jnp.float32
    )


def tiles(total, size):
    size = min(size, total)
    return [(start, size) for start in range(0, total, size)]


def seen(step, base_ref, pos_ref, span, tile, width):
    key_pos = base_ref[0] + step * tile + lax.broadcasted_iota(jnp.int32, (tile, width), 0)
    return key_pos <= pos_ref[:, span]


def fold(parts_ref, span):
    result = []
    for row in (0, 2):
        logs = [parts_ref[part, row : row + 1, span] for part in range(parts_ref.shape[0])]
        means = [parts_ref[part, row + 1 : row + 2, span] for part in range(parts_ref.shape[0])]
        top = logs[0]
        for item in logs[1:]:
            top = jnp.maximum(top, item)
        total, mix = jnp.zeros_like(top), jnp.zeros_like(top)
        for item, mean in zip(logs, means):
            weight = jnp.exp(item - top)
            total = total + weight
            mix = mix + weight * mean
        result.append((top + jnp.log(total), mix / total))
    return result


def stats_kernel(
    base_ref, pos_ref, every_ref, k_one_ref, k_two_ref, val_ref, stats_ref, run_ref
):
    tile, head_dim = k_one_ref.shape
    scale = head_dim**-0.5
    step = pl.program_id(0)

    @pl.when(step == 0)
    def _():
        row = lax.broadcasted_iota(jnp.int32, run_ref.shape, 0)
        run_ref[...] = jnp.where((row == 0) | (row == 4), NEG, 0.0)

    for start, width in tiles(every_ref.shape[0], ROW_TILE):
        span = slice(start, start + width)
        visible = seen(step, base_ref, pos_ref, span, tile, width)
        product = outer(val_ref[...], every_ref[span, 2 * head_dim :])
        for row, k_ref, offset in ((0, k_one_ref, 0), (4, k_two_ref, head_dim)):
            logits = outer(k_ref[...], every_ref[span, offset : offset + head_dim]) * scale
            logits = jnp.where(visible, logits, NEG)
            before = run_ref[row : row + 1, span]
            top = jnp.maximum(before, jnp.max(logits, axis=0, keepdims=True))
            expo = jnp.exp(logits - top)
            kept = jnp.exp(before - top)
            run_ref[row : row + 1, span] = top
            run_ref[row + 1 : row + 2, span] = run_ref[
                row + 1 : row + 2, span
            ] * kept + jnp.sum(expo, axis=0, keepdims=True)
            run_ref[row + 2 : row + 3, span] = run_ref[
                row + 2 : row + 3, span
            ] * kept + jnp.sum(expo * product, axis=0, keepdims=True)

    @pl.when(step == pl.num_programs(0) - 1)
    def _():
        for row in (0, 4):
            log = run_ref[row : row + 1, :] + jnp.log(run_ref[row + 1 : row + 2, :])
            mean = run_ref[row + 2 : row + 3, :] / run_ref[row + 1 : row + 2, :]
            stats_ref[row // 2 : row // 2 + 1, :] = log
            stats_ref[row // 2 + 1 : row // 2 + 2, :] = mean


def fold_kernel(parts_ref, out_ref):
    (log_one, mean_one), (log_two, mean_two) = fold(parts_ref, slice(None))
    out_ref[0:1, :] = log_one
    out_ref[1:2, :] = mean_one
    out_ref[2:3, :] = log_two
    out_ref[3:4, :] = mean_two


def query_kernel(
    base_ref,
    lam_ref,
    pos_ref,
    far_ref,
    every_ref,
    k_one_ref,
    k_two_ref,
    val_ref,
    out_ref,
    final_ref,
    acc_ref,
):
    tile, head_dim = k_one_ref.shape
    scale = head_dim**-0.5
    step = pl.program_id(0)

    @pl.when(step == 0)
    def _():
        fold_kernel(far_ref, final_ref)
        acc_ref[...] = jnp.zeros_like(acc_ref)

    for start, width in tiles(every_ref.shape[0], ROW_TILE):
        span = slice(start, start + width)
        visible = seen(step, base_ref, pos_ref, span, tile, width)
        product = outer(val_ref[...], every_ref[span, 2 * head_dim :])
        for number, k_ref, factor in ((0, k_one_ref, scale), (1, k_two_ref, -lam_ref[0] * scale)):
            top = number * head_dim
            log = final_ref[2 * number : 2 * number + 1, span]
            mean = final_ref[2 * number + 1 : 2 * number + 2, span]
            logits = outer(k_ref[...], every_ref[span, top : top + head_dim]) * scale
            prob = jnp.exp(jnp.where(visible, logits, NEG) - log)
            slope = (prob * (product - mean) * factor).astype(jnp.bfloat16)
            acc_ref[top : top + head_dim, span] += matmul_first(k_ref[...], slope)

    @pl.when(step == pl.num_programs(0) - 1)
    def _():
        out_ref[...] = acc_ref[...].T.astype(jnp.bfloat16)


def key_kernel(
    base_ref,
    lam_ref,
    pos_ref,
    far_ref,
    every_ref,
    k_one_ref,
    k_two_ref,
    val_ref,
    dk_one_ref,
    dk_two_ref,
    dval_ref,
    final_ref,
):
    tile, head_dim = k_one_ref.shape
    scale = head_dim**-0.5
    step = pl.program_id(0)
    lam = lam_ref[0]

    @pl.when(step == 0)
    def _():
        fold_kernel(far_ref, final_ref)

    grad_one = jnp.zeros((tile, head_dim), jnp.float32)
    grad_two = jnp.zeros((tile, head_dim), jnp.float32)
    grad_val = jnp.zeros((tile, 2 * head_dim), jnp.float32)
    for start, width in tiles(every_ref.shape[0], ROW_TILE):
        span = slice(start, start + width)
        visible = seen(step, base_ref, pos_ref, span, tile, width)
        q_one = every_ref[span, :head_dim]
        q_two = every_ref[span, head_dim : 2 * head_dim]
        cotangent = every_ref[span, 2 * head_dim :]
        product = outer(val_ref[...], cotangent)
        logits_one = jnp.where(visible, outer(k_one_ref[...], q_one) * scale, NEG)
        logits_two = jnp.where(visible, outer(k_two_ref[...], q_two) * scale, NEG)
        prob_one = jnp.exp(logits_one - final_ref[0:1, span])
        prob_two = jnp.exp(logits_two - final_ref[2:3, span]) * lam
        mixed = (prob_one - prob_two).astype(jnp.bfloat16)
        slope_one = (prob_one * (product - final_ref[1:2, span]) * scale).astype(jnp.bfloat16)
        slope_two = (prob_two * (final_ref[3:4, span] - product) * scale).astype(jnp.bfloat16)
        grad_val = grad_val + matmul(mixed, cotangent)
        grad_one = grad_one + matmul(slope_one, q_one)
        grad_two = grad_two + matmul(slope_two, q_two)
    dk_one_ref[...] = grad_one.astype(jnp.bfloat16)
    dk_two_ref[...] = grad_two.astype(jnp.bfloat16)
    dval_ref[...] = grad_val.astype(jnp.bfloat16)


def whole(shape):
    return pl.BlockSpec(shape, lambda step: (0,) * len(shape))


def keyed(width):
    return pl.BlockSpec((KEY_TILE, width), lambda step: (step, 0))


SMEM = pl.BlockSpec(memory_space=pltpu.SMEM)


def over_keys(kernel, scalars, fixed, keyed_in, fixed_out, keyed_out, scratch, flops):
    keys = keyed_in[0].shape[0]
    outs = fixed_out + tuple(jax.ShapeDtypeStruct((keys, w), jnp.bfloat16) for w in keyed_out)
    return pl.pallas_call(
        kernel,
        grid=(keys // KEY_TILE,),
        out_shape=outs,
        in_specs=[SMEM] * len(scalars)
        + [whole(item.shape) for item in fixed]
        + [keyed(item.shape[1]) for item in keyed_in],
        out_specs=tuple(whole(item.shape) for item in fixed_out)
        + tuple(keyed(w) for w in keyed_out),
        scratch_shapes=[pltpu.VMEM(shape, jnp.float32) for shape in scratch],
        compiler_params=VMEM,
        cost_estimate=pl.CostEstimate(
            flops=flops, bytes_accessed=4 * 1024 * 1024, transcendentals=flops // 512
        ),
    )(*scalars, *fixed, *keyed_in)


def spread(value, axes):
    copies = jnp.broadcast_to(value[None], (lax.axis_size(axes),) + value.shape)
    return lax.all_to_all(copies, axes, 0, 0)


def body(sizes, q_first, q_second, grad_out, k_first, k_second, values, w_query, offsets, lam):
    rows_own, head_dim = q_first.shape
    keys_own = k_first.shape[0]
    y, z, core = (sizes[name] for name in ("y", "z", "core"))
    rows = y * z * core * rows_own
    base = (lax.axis_index(("y", "z", "core")) * keys_own).astype(jnp.int32).reshape(1)
    starts = offsets.reshape(y, z, core).transpose(0, 2, 1).reshape(-1, 1) * rows_own
    positions = (starts + jnp.arange(rows_own, dtype=jnp.int32)[None, :]).reshape(1, rows)

    own = jnp.concatenate([q_first, q_second, grad_out], axis=1)
    every = spread(lax.all_gather(own, "z"), ("y", "core")).reshape(rows, 4 * head_dim)

    held = (k_first, k_second, values)
    pairs = rows * keys_own * head_dim
    stats_of = jax.ShapeDtypeStruct((STATS, rows), jnp.float32)
    (stats,) = over_keys(
        stats_kernel, (base,), (positions, every), held, (stats_of,), (), [(8, rows)], 8 * pairs
    )
    stats = lax.all_gather(stats, ("y", "core"))
    stats = pl.pallas_call(fold_kernel, out_shape=stats_of, compiler_params=VMEM)(stats)
    stats = lax.all_gather(stats, "z")
    (dq,) = over_keys(
        query_kernel,
        (base, lam),
        (positions, stats, every),
        held,
        (jax.ShapeDtypeStruct((rows, 2 * head_dim), jnp.bfloat16),),
        (),
        [(STATS, rows), (2 * head_dim, rows)],
        12 * pairs,
    )
    dq = dq.reshape(y * core, z * rows_own, 2 * head_dim)
    dq = lax.all_to_all(dq, ("y", "core"), 0, 0)
    dk_first, dk_second, dval = over_keys(
        key_kernel,
        (base, lam),
        (positions, stats, every),
        held,
        (),
        (head_dim, head_dim, 2 * head_dim),
        [(STATS, rows)],
        16 * pairs,
    )
    dq = jnp.sum(dq.astype(jnp.float32), axis=0).astype(jnp.bfloat16)
    dq = lax.all_to_all(dq.reshape(z, rows_own, 2 * head_dim), "z", 0, 0)
    dq = jnp.sum(dq.astype(jnp.float32), axis=0).astype(jnp.bfloat16)

    heads = sizes["head"]
    columns = w_query.reshape(heads, w_query.shape[0] // heads, 2 * head_dim)
    term = jnp.einsum("qe,hde->hqd", dq, columns, preferred_element_type=jnp.float32)
    term = lax.all_to_all(term.astype(jnp.bfloat16), "head", 0, 0)
    slab = jnp.sum(term.astype(jnp.float32), axis=0).astype(jnp.bfloat16)
    return dq[:, :head_dim], dq[:, head_dim:], dk_first, dk_second, dval, slab


def build(mesh, y, z, core):
    names = ("y", "z", "core", "head")
    fine = Mesh(mesh.devices.reshape(y, z, core, mesh.shape["head"]), names)
    sizes = dict(zip(names, fine.devices.shape))
    cut = P(("y", "z", "core"), "head")

    def run(*args):
        return body(sizes, *args)

    return jax.shard_map(
        run,
        mesh=fine,
        in_specs=(cut,) * 6 + (P(None, "head"), P(), P()),
        out_specs=(cut,) * 6,
        check_vma=False,
    )


def solution(mesh):
    return build(mesh, 4, 8, 2)
```
